32 devices in a mesh: gz: 4 (over x, core), xy: 8 (over z, y).
Axes of the slice: x: 2, y: 2, z: 4, core: 2. Of those that a mesh axis runs over, the one named last changes fastest.
Arguments:
- adjoint_e: float32 [3, 56, 128, 128], P(None, 'gz', 'xy'), may hold values from -6 to 6
- adjoint_h: float32 [3, 56, 128, 128], P(None, 'gz', 'xy'), may hold values from -6 to 6
- source_e: bfloat16 [3, 56, 128, 128], P(None, 'gz', 'xy'), may hold values from -6 to 6
- e_saved: bfloat16 [3, 3, 56, 128, 128], P(None, None, 'gz', 'xy'), may hold values from -6 to 6
- material_eps: float32 [8], replicated, may hold values from 1 to 12
- material_id: int32 [56, 128, 128], P('gz', 'xy'), may hold values from 0 to 7
- pml_level: int32 [56, 128, 128], P('gz', 'xy'), may hold values from 0 to 3
- block_map: int32 [128, 128], P('xy'), may hold values from 0 to 64, as said below
Outputs:
- field_e: float32 [3, 56, 128, 128], P(None, 'gz', 'xy')
- field_h: float32 [3, 56, 128, 128], P(None, 'gz', 'xy')
- design_grad: float32 [64], P(('gz', 'xy'))
The draws below stay inside these ranges and needn't reach their ends.
Inputs may be any that keep to these rules, and one draw needn't show every extreme that they name: block_map is constant over aligned groups of 4 x 4 columns; every value from 0 to 64 occurs.
All inputs are finite; a program needn't handle non-finite values.
Results may differ from the reference program's by a relative error of at most 0.0004.
Values sent between devices are 32-bit elements; how exact they have to be, the bound alone decides.
No kernel may reach another device: no remote copies, remote signals or barrier semaphores. Data moves between devices by JAX's collectives and lax.ppermute only.
A program may use at most 64 MiB of HBM per device.

```python
import math
import jax
import jax.numpy as jnp
from jax import lax

NY = 128
MATS = 8
NZ = 56
NX = 128
NB = 64


def draw_block_map(key, part):
    groups = jax.random.permutation(key, NX // 4 * (NY // 4))
    labels = groups % (NB + NB // 2)
    labels = jnp.where(labels >= NB, NB, labels).astype(jnp.int32)
    labels = labels.reshape(NX // 4, NY // 4)
    return jnp.repeat(jnp.repeat(labels, 4, axis=0), 4, axis=1)


def plant(array, stream_key, smallest, top_value):
    place = [jax.random.randint(jax.random.fold_in(stream_key, axis), (), 0, length) for axis, length in enumerate(array.shape)]
    main_axis = array.shape.index(max(array.shape))
    beside = place[:main_axis] + [(place[main_axis] + 1) % array.shape[main_axis]] + place[main_axis + 1:]
    return array.at[tuple(place)].set(smallest).at[tuple(beside)].set(top_value)


def block_scale(own_key, shape, cuts, least, largest):
    loudness, own = 1.0, jax.random.fold_in(own_key, 6)
    for position, shards_of in cuts:
        draws = jnp.exp(jax.random.uniform(jax.random.fold_in(own, position), (shards_of,), jnp.float32, least / len(cuts), largest / len(cuts)))
        loudness = loudness * jnp.repeat(draws, shape[position] // shards_of).reshape([-1 if axis == position else 1 for axis in range(len(shape))])
    return loudness


def scatter_about(stream_key, extent, deviation, most, split=(), dtype=jnp.bfloat16):
    drawn = deviation * jax.random.normal(stream_key, extent, jnp.float32)
    if split:
        drawn = drawn * block_scale(stream_key, extent, split, -0.22, 0.18)
    return jnp.clip(drawn, -most, most).astype(dtype)


def setup_inputs(seed: int = 0) -> dict:
    streams_of = jax.random.split(jax.random.key(seed), 9)
    return {
        "adjoint_e": scatter_about(streams_of[0], (3, NZ, NX, NY), 1.0, 6.0, ((1, 4), (2, 8)), jnp.float32),
        "adjoint_h": scatter_about(streams_of[1], (3, NZ, NX, NY), 1.0, 6.0, ((1, 4), (2, 8)), jnp.float32),
        "source_e": scatter_about(streams_of[2], (3, NZ, NX, NY), 1.0, 6.0, ((1, 4), (2, 8))),
        "e_saved": scatter_about(streams_of[3], (3, 3, NZ, NX, NY), 1.0, 6.0, ((2, 4), (3, 8))),
        "material_eps": jnp.clip(jnp.exp(jax.random.uniform(streams_of[4], (MATS,), jnp.float32, math.log(1.0), math.log(12.0))), 1.0, 12.0),
        "material_id": plant(jax.random.randint(streams_of[5], (NZ, NX, NY), 0, MATS), jax.random.fold_in(streams_of[5], 1), 0, MATS - 1).astype(jnp.int32),
        "pml_level": plant(jax.random.randint(streams_of[6], (NZ, NX, NY), 0, 4), jax.random.fold_in(streams_of[6], 1), 0, 3).astype(jnp.int32),
        "block_map": draw_block_map(jax.random.fold_in(streams_of[8], 71), 0),
    }


DT_STEP = 0.5
SIGMA_UNIT = 0.15


def step_next(field, axis):
    count = field.shape[axis]
    upper = lax.slice_in_dim(field, 1, count, axis=axis)
    zero_row = jnp.zeros_like(lax.slice_in_dim(field, 0, 1, axis=axis))
    return jnp.concatenate([upper, zero_row], axis=axis) - field


def step_prev(field, axis):
    count = field.shape[axis]
    lower = lax.slice_in_dim(field, 0, count - 1, axis=axis)
    zero_row = jnp.zeros_like(lax.slice_in_dim(field, 0, 1, axis=axis))
    return field - jnp.concatenate([zero_row, lower], axis=axis)


def curl_of(field, differ):
    comp_x, comp_y, comp_z = field[0], field[1], field[2]
    out_x = differ(comp_z, 2) - differ(comp_y, 0)
    out_y = differ(comp_x, 0) - differ(comp_z, 1)
    out_z = differ(comp_y, 1) - differ(comp_x, 2)
    return jnp.stack([out_x, out_y, out_z], 0)


def reference(adjoint_e, adjoint_h, source_e, e_saved, material_eps, material_id, pml_level, block_map):
    permit = material_eps[material_id]
    sigma = SIGMA_UNIT * pml_level.astype(jnp.float32)
    decay = (1.0 - sigma) / (1.0 + sigma)
    drive = DT_STEP / (permit * (1.0 + sigma))
    source = source_e.astype(jnp.float32)
    field_e = adjoint_e
    field_h = adjoint_h
    cell_grad = jnp.zeros(permit.shape, jnp.float32)
    for section in range(2):
        incoming = field_e + source
        after = e_saved[2 - section].astype(jnp.float32)
        before = e_saved[1 - section].astype(jnp.float32)
        cell_grad = cell_grad - jnp.sum(incoming * (after - decay * before), 0) / permit
        field_h = field_h + curl_of(drive * incoming, step_next)
        field_e = decay * incoming - DT_STEP * curl_of(field_h, step_prev)
    columns = jnp.sum(cell_grad, 0) / NZ
    design_grad = jax.ops.segment_sum(columns.reshape(-1), block_map.reshape(-1).astype(jnp.int32), num_segments=NB + 1)[:NB]
    return field_e, field_h, design_grad
```

```python
import functools

import jax
import jax.numpy as jnp
from jax import lax
from jax.experimental import pallas as pl
from jax.experimental.pallas import tpu as pltpu
from jax.sharding import PartitionSpec as P

B_DEV = 2

DT_STEP = 0.5
SIGMA_UNIT = 0.15

V0, V1, V2, Q0, Q1, Q2, DR, H0, H1, H2 = range(10)
DECAY, INV = 7, 8
ALL = tuple(range(10))

Z_TOP = [(c, -1) for c in ALL] + [(c, -2) for c in (V0, V1, V2, H0, H1)]
Z_BOT = [(c, 0) for c in (V0, V1, V2, Q0, Q1, DR, H0, H1, H2)] + [(V0, 1), (V1, 1)]
X_TOP = [(c, -1) for c in ALL] + [(c, -2) for c in (V0, V1, V2, H1, H2)]
X_BOT = [(c, 0) for c in (V0, V1, V2, Q1, Q2, DR, H0, H1, H2)] + [(V1, 1), (V2, 1)]
SLOTS = len(Z_TOP)

VMEM = pl.BlockSpec(memory_space=pltpu.VMEM)
SMEM = pl.BlockSpec(memory_space=pltpu.SMEM)
ANY = pl.BlockSpec(memory_space=pl.ANY)


def round_up(value, unit):
    return -(-value // unit) * unit


def prepare_kernel(nz, nx, eps, e, h, s, mat, pml, vqd, za, zb, xa, xb):
    cells = nz * nx
    inverse = [1.0 / jnp.full((nx, 128), eps[k], jnp.float32) for k in range(eps.shape[0])]
    for z in range(nz):
        rows = pl.ds(z * nx, nx)
        kind = mat[rows, :]
        inv = inverse[0]
        for k in range(1, len(inverse)):
            inv = jnp.where(kind == k, inverse[k], inv)
        sigma = SIGMA_UNIT * pml[rows, :].astype(jnp.float32)
        recip = 1.0 / (1.0 + sigma)
        decay = (1.0 - sigma) * recip
        drive = DT_STEP * inv * recip
        vqd[pl.ds(DR * cells + z * nx, nx), :] = drive
        vqd[pl.ds(DECAY * cells + z * nx, nx), :] = decay
        vqd[pl.ds(INV * cells + z * nx, nx), :] = inv
        for c in range(3):
            at = pl.ds(c * cells + z * nx, nx)
            source = s[at, :].astype(jnp.float32)
            incoming = e[at, :] + source
            vqd[at, :] = drive * incoming
            vqd[pl.ds((Q0 + c) * cells + z * nx, nx), :] = decay * incoming + source

    def layer(c, z):
        if c < H0:
            return vqd[pl.ds(c * cells + z * nx, nx), :]
        return h[pl.ds((c - H0) * cells + z * nx, nx), :]

    def column(c, x):
        if c < H0:
            return vqd[pl.ds(c * cells + x, nz, stride=nx), :]
        return h[pl.ds((c - H0) * cells + x, nz, stride=nx), :]

    def pack_z(top, bottom):
        for slot, (c, dz) in enumerate(Z_TOP):
            top[pl.ds(slot * nx, nx), :] = layer(c, nz + dz)
        for slot, (c, dz) in enumerate(Z_BOT):
            bottom[pl.ds(slot * nx, nx), :] = layer(c, dz)

    def pack_x(top, bottom):
        for slot, (c, dx) in enumerate(X_TOP):
            top[pl.ds(slot * nz, nz), :] = column(c, nx + dx)
        for slot, (c, dx) in enumerate(X_BOT):
            bottom[pl.ds(slot * nz, nz), :] = column(c, dx)

    odd_z = lax.rem(lax.axis_index("gz"), 2) == 1
    odd_x = lax.rem(lax.axis_index("xy"), 2) == 1
    for odd, pack, first, second in ((odd_z, pack_z, za, zb), (odd_x, pack_x, xa, xb)):
        pl.when(jnp.logical_not(odd))(functools.partial(pack, first, second))
        pl.when(odd)(functools.partial(pack, second, first))


def corner_kernel(nz, nx, za, zb, xa_in, xb_in, xa, xb, top, bottom, sems):
    base = round_up(SLOTS * nz, 8)

    def gather(low, high):
        for slots, out in ((X_TOP, top), (X_BOT, bottom)):
            for slot, (c, dx) in enumerate(slots):
                x = dx if dx >= 0 else nx + dx
                for k, (ref, sent, dz) in enumerate(
                    ((low, Z_TOP, -2), (low, Z_TOP, -1), (high, Z_BOT, 0), (high, Z_BOT, 1))
                ):
                    if (c, dz) in sent:
                        row = sent.index((c, dz)) * nx + x
                        out[pl.ds(slot * 4 + k, 1), :] = ref[pl.ds(row, 1), :]

    odd_z = lax.rem(lax.axis_index("gz"), 2) == 1
    odd_x = lax.rem(lax.axis_index("xy"), 2) == 1
    pl.when(jnp.logical_not(odd_z))(functools.partial(gather, zb, za))
    pl.when(odd_z)(functools.partial(gather, za, zb))

    def put(first, second):
        window = pl.ds(base, top.shape[0])
        one = pltpu.make_async_copy(first, xa.at[window, :], sems.at[0])
        two = pltpu.make_async_copy(second, xb.at[window, :], sems.at[1])
        one.start()
        two.start()
        one.wait()
        two.wait()

    pl.when(jnp.logical_not(odd_x))(functools.partial(put, top, bottom))
    pl.when(odd_x)(functools.partial(put, bottom, top))


def weight_kernel(nz, nx, e, s, saved, vqd, weight, column):
    cells = nz * nx
    total = jnp.zeros((nx, 128), jnp.float32)
    for z in range(nz):
        decay = vqd[pl.ds(DECAY * cells + z * nx, nx), :]
        inv = vqd[pl.ds(INV * cells + z * nx, nx), :]
        cell = jnp.zeros((nx, 128), jnp.float32)
        for c in range(3):
            at = pl.ds(c * cells + z * nx, nx)
            times = [
                saved[pl.ds((3 * t + c) * cells + z * nx, nx), :].astype(jnp.float32)
                for t in range(3)
            ]
            incoming = e[at, :] + s[at, :].astype(jnp.float32)
            cell = cell + incoming * (times[2] - decay * times[1])
            weight[at, :] = (times[1] - decay * times[0]) * inv
        total = total + cell * inv
    column[...] = total


def march_kernel(
    nz, nx, layers, vqd, h, weight, column, za, zb, xa, xb, blocks, out_e, out_h, sums, zh, xh
):
    cells = nz * nx
    base = round_up(SLOTS * nz, 8)
    deep = nz + 4
    index_z, index_x = lax.axis_index("gz"), lax.axis_index("xy")
    odd_z, odd_x = lax.rem(index_z, 2) == 1, lax.rem(index_x, 2) == 1

    def take_z(low, high):
        zh[pl.ds(0, SLOTS * nx), :] = low[...]
        zh[pl.ds(SLOTS * nx, len(Z_BOT) * nx), :] = high[pl.ds(0, len(Z_BOT) * nx), :]

    def take_x(low, high):
        for slots, ref in ((X_TOP, low), (X_BOT, high)):
            for slot, (c, dx) in enumerate(slots):
                place = c * deep * 8 + dx % 8
                xh[pl.ds(place + 16, nz, stride=8), :] = ref[pl.ds(slot * nz, nz), :]
                xh[pl.ds(place, 2, stride=8), :] = ref[pl.ds(base + slot * 4, 2), :]
                upper = ref[pl.ds(base + slot * 4 + 2, 2), :]
                xh[pl.ds(place + (nz + 2) * 8, 2, stride=8), :] = upper

    pl.when(jnp.logical_not(odd_z))(functools.partial(take_z, zb, za))
    pl.when(odd_z)(functools.partial(take_z, za, zb))
    pl.when(jnp.logical_not(odd_x))(functools.partial(take_x, xb, xa))
    pl.when(odd_x)(functools.partial(take_x, xa, xb))

    tall = nx + 8
    lane = lax.broadcasted_iota(jnp.int32, (tall, 128), 1)
    row = lax.broadcasted_iota(jnp.int32, (tall, 128), 0)
    last, first = lane == 127, lane == 0
    inside_x = jnp.logical_or(row < nx + 4, jnp.broadcast_to(index_x, (tall, 128)) > 0)
    inside_z = jnp.logical_and(inside_x, jnp.broadcast_to(index_z, (tall, 128)) > 0)

    def load(c, z):
        side = xh[pl.ds((c * deep + z + 2) * 8, 8), :]
        if z < 0:
            own = zh[pl.ds(Z_TOP.index((c, z)) * nx, nx), :]
        elif z >= nz:
            own = zh[pl.ds((SLOTS + Z_BOT.index((c, z - nz))) * nx, nx), :]
        elif c < H0:
            own = vqd[pl.ds(c * cells + z * nx, nx), :]
        else:
            own = h[pl.ds((c - H0) * cells + z * nx, nx), :]
        return jnp.concatenate([own, side], axis=0)

    def next_y(f):
        return jnp.where(last, 0.0, pltpu.roll(f, 127, 1)) - f

    def prev_y(f):
        return f - jnp.where(first, 0.0, pltpu.roll(f, 1, 1))

    def next_x(f):
        return pltpu.roll(f, tall - 1, 0) - f

    def prev_x(f):
        return f - pltpu.roll(f, 1, 0)

    def magnetic(z, old, here, above, want_z):
        keep = inside_z if z < 0 else inside_x
        out = [
            old[0] + (next_y(here[2]) - (above[1] - here[1])),
            old[1] + ((above[0] - here[0]) - next_x(here[2])),
        ]
        if want_z:
            out.append(old[2] + (next_x(here[1]) - next_y(here[0])))
        return [jnp.where(keep, f, 0.0) for f in out]

    def curl_p(here, below, want_z):
        out = [
            prev_y(here[2]) - (here[1] - below[1]),
            (here[0] - below[0]) - prev_x(here[2]),
        ]
        if want_z:
            out.append(prev_x(here[1]) - prev_y(here[0]))
        return out

    total = column[...]
    v_here = [load(c, -2) for c in (V0, V1, V2)]
    mag_below, mag2_below = None, None
    inc_below, drv_below, mag_mid = None, None, None
    for z in range(-2, nz + 1):
        v_above = [load(c, z + 1) for c in ((V0, V1, V2) if z < nz else (V0, V1))]
        comps = (H0, H1) if z == -2 else (H0, H1, H2)
        mag = magnetic(z, [load(c, z) for c in comps], v_here, v_above, z > -2)
        v_here = v_above
        if z > -2:
            full = z < nz
            curl = curl_p(mag, mag_below, full)
            inc = [load(Q0 + c, z) - DT_STEP * curl[c] for c in range(3 if full else 2)]
            drive = load(DR, z)
            drv = [drive * f for f in inc]
            if 0 <= z < nz:
                cell = jnp.zeros((nx, 128), jnp.float32)
                for c in range(3):
                    cell = cell + inc[c][:nx] * weight[pl.ds(c * cells + z * nx, nx), :]
                total = total + cell
            if z > -1:
                low = z - 1
                mag2 = magnetic(low, mag_mid, drv_below, drv, low >= 0)
                if low >= 0:
                    decay = vqd[pl.ds(DECAY * cells + low * nx, nx), :]
                    curl = curl_p(mag2, mag2_below, True)
                    for c in range(3):
                        at = pl.ds(c * cells + low * nx, nx)
                        out_h[at, :] = mag2[c][:nx]
                        out_e[at, :] = decay * inc_below[c][:nx] - DT_STEP * curl[c][:nx]
                mag2_below = mag2
            inc_below, drv_below = inc, drv
        mag_mid, mag_below = mag, mag

    devices = sums.shape[0]
    total = total * (-1.0 / layers)
    owner = B_DEV * lax.broadcasted_iota(jnp.int32, (devices, 128), 0)
    spot = lax.broadcasted_iota(jnp.int32, (devices, 128), 1)
    parts = [jnp.zeros((devices, 128), jnp.float32) for _ in range(B_DEV)]
    for group in range(nx // 4):
        four = jnp.sum(total[4 * group : 4 * group + 4], axis=0, keepdims=True)
        label = blocks[pl.ds(4 * group, 1), :]
        for k in range(B_DEV):
            parts[k] = parts[k] + jnp.where(label == owner + k, four, 0.0)
    packed = jnp.zeros((devices, 128), jnp.float32)
    for k in range(B_DEV):
        packed = jnp.where(spot == k, jnp.sum(parts[k], axis=1, keepdims=True), packed)
    sums[...] = packed


def swap_pairs(count, offset):
    pairs = []
    for low in range(offset, count - 1, 2):
        pairs += [(low, low + 1), (low + 1, low)]
    return pairs


def estimate(flops, moved):
    return pl.CostEstimate(flops=flops, bytes_accessed=moved, transcendentals=0)


def on_device(
    adjoint_e, adjoint_h, source_e, e_saved, material_eps, material_id, pml_level, block_map
):
    nz, nx, ny = material_id.shape
    slabs, tiles = lax.axis_size("gz"), lax.axis_size("xy")
    cells = nz * nx
    f32 = jnp.float32
    flat = lambda a: a.reshape(-1, ny)
    e, h, s, saved = flat(adjoint_e), flat(adjoint_h), flat(source_e), flat(e_saved)
    mat, pml = flat(material_id), flat(pml_level)
    base = round_up(SLOTS * nz, 8)
    corner = round_up(SLOTS * 4, 8)
    z_msg = jax.ShapeDtypeStruct((SLOTS * nx, ny), f32)
    x_msg = jax.ShapeDtypeStruct((base + corner, ny), f32)
    params = pltpu.CompilerParams(vmem_limit_bytes=24 * 1024 * 1024)

    vqd, za, zb, xa, xb = pl.pallas_call(
        functools.partial(prepare_kernel, nz, nx),
        out_shape=(jax.ShapeDtypeStruct((9 * cells, ny), f32), z_msg, z_msg, x_msg, x_msg),
        in_specs=[SMEM] + [VMEM] * 5,
        out_specs=(VMEM,) * 5,
        compiler_params=params,
        cost_estimate=estimate(60 * cells * ny, 4 * 20 * cells * ny),
        name="prepare",
    )(material_eps, e, h, s, mat, pml)

    za = lax.ppermute(za, "gz", swap_pairs(slabs, 0))
    zb = lax.ppermute(zb, "gz", swap_pairs(slabs, 1))

    weight, column = pl.pallas_call(
        functools.partial(weight_kernel, nz, nx),
        out_shape=(
            jax.ShapeDtypeStruct((3 * cells, ny), f32),
            jax.ShapeDtypeStruct((nx, ny), f32),
        ),
        in_specs=[VMEM] * 4,
        out_specs=(VMEM,) * 2,
        compiler_params=params,
        cost_estimate=estimate(40 * cells * ny, 4 * 16 * cells * ny),
        name="weights",
    )(e, s, saved, vqd)

    xa, xb = pl.pallas_call(
        functools.partial(corner_kernel, nz, nx),
        out_shape=(x_msg, x_msg),
        in_specs=[VMEM, VMEM, ANY, ANY],
        out_specs=(ANY, ANY),
        scratch_shapes=[
            pltpu.VMEM((corner, ny), f32),
            pltpu.VMEM((corner, ny), f32),
            pltpu.SemaphoreType.DMA((2,)),
        ],
        input_output_aliases={2: 0, 3: 1},
        compiler_params=params,
        cost_estimate=estimate(cells * ny, 4 * cells * ny),
        name="corners",
    )(za, zb, xa, xb)

    xa = lax.ppermute(xa, "xy", swap_pairs(tiles, 0))
    xb = lax.ppermute(xb, "xy", swap_pairs(tiles, 1))

    field_e, field_h, sums = pl.pallas_call(
        functools.partial(march_kernel, nz, nx, nz * slabs),
        out_shape=(
            jax.ShapeDtypeStruct((3 * cells, ny), f32),
            jax.ShapeDtypeStruct((3 * cells, ny), f32),
            jax.ShapeDtypeStruct((slabs * tiles, ny), f32),
        ),
        in_specs=[VMEM] * 9,
        out_specs=(VMEM,) * 3,
        scratch_shapes=[
            pltpu.VMEM(((SLOTS + len(Z_BOT)) * nx, ny), f32),
            pltpu.VMEM((10 * (nz + 4) * 8, ny), f32),
        ],
        compiler_params=params,
        cost_estimate=estimate(200 * cells * ny, 4 * 30 * cells * ny),
        name="march",
    )(vqd, h, weight, column, za, zb, xa, xb, block_map)

    gathered = lax.all_to_all(sums, ("gz", "xy"), 0, 0, tiled=True)
    design_grad = jnp.sum(gathered, axis=0)[:B_DEV]
    return field_e.reshape(adjoint_e.shape), field_h.reshape(adjoint_h.shape), design_grad


def solution(mesh):
    placed = (
        P(None, "gz", "xy", None),
        P(None, "gz", "xy", None),
        P(None, "gz", "xy", None),
        P(None, None, "gz", "xy", None),
        P(),
        P("gz", "xy", None),
        P("gz", "xy", None),
        P("xy", None),
    )
    return jax.shard_map(
        on_device,
        mesh=mesh,
        in_specs=placed,
        out_specs=(P(None, "gz", "xy", None), P(None, "gz", "xy", None), P(("gz", "xy"))),
        check_vma=False,
    )
```

```python
import functools

import jax
import jax.numpy as jnp
from jax import lax
from jax.experimental import pallas as pl
from jax.experimental.pallas import tpu as pltpu
from jax.sharding import PartitionSpec as P

B_DEV = 2

DT_STEP = 0.5
SIGMA_UNIT = 0.15

V0, V1, V2, Q0, Q1, Q2, DR, H0, H1, H2, I0, I1, I2, DECAY, INV = range(15)
FIELDS = 15

Z_LOW = (H0, H1, H2, Q0, Q1, Q2, DR)
Z_HIGH = (V0, V1, V2, Q0, Q1, DR, H1, H2)
X_LOW = (H1, H2, Q0, Q1, Q2, DR)
X_HIGH = (V1, V2, Q1, Q2, DR)
EXTRA_Z = 7
EXTRA_X = 5
Z_SLOTS, X_SLOTS = 8, 6

VMEM = pl.BlockSpec(memory_space=pltpu.VMEM)
HBM = pl.BlockSpec(memory_space=pltpu.HBM)


def shape_of(rows, ny):
    return jax.ShapeDtypeStruct((rows, ny), jnp.float32)


def is_odd(axis):
    return lax.rem(lax.axis_index(axis), 2) == 1


def either(odd, body, first, second):
    pl.when(jnp.logical_not(odd))(functools.partial(body, first, second))
    pl.when(odd)(functools.partial(body, second, first))


def masks(tall):
    row = lax.broadcasted_iota(jnp.int32, (tall, 128), 0)
    lane = lax.broadcasted_iota(jnp.int32, (tall, 128), 1)
    return row, lane == 0, lane == 127


def inverse_table(eps, nx):
    return [1.0 / jnp.full((nx, 128), eps[k], jnp.float32) for k in range(eps.shape[0])]


def cell_factors(kind, level, table):
    inv = table[0]
    for k in range(1, len(table)):
        inv = jnp.where(kind == k, table[k], inv)
    sigma = SIGMA_UNIT * level.astype(jnp.float32)
    recip = 1.0 / (1.0 + sigma)
    return (1.0 - sigma) * recip, DT_STEP * inv * recip, inv


def faces_kernel(nz, nx, eps_in, e_in, h_in, s_in, mat_in, pml_in, za, zb, eps, *rest):
    bufs, sems = rest[:-1], rest[-1]
    copies = [pltpu.make_async_copy(eps_in, eps, sems.at[0])]
    for k, ref in enumerate((e_in, h_in, s_in, mat_in, pml_in)):
        for side, start in enumerate((0, nz - 2)):
            part = pl.ds(start, 2)
            source = ref.at[:, part] if k < 3 else ref.at[part]
            copies.append(pltpu.make_async_copy(source, bufs[k].at[side], sems.at[len(copies)]))
    for copy in copies:
        copy.start()
    for copy in copies:
        copy.wait()
    e, h, s, mat, pml = bufs
    table = inverse_table(eps, nx)
    row, first, last = masks(nx)

    def next_y(f):
        return jnp.where(last, 0.0, pltpu.roll(f, 127, 1)) - f

    def next_x(f):
        return jnp.where(row == nx - 1, 0.0, pltpu.roll(f, nx - 1, 0)) - f

    def layer(side, z):
        decay, drive, _ = cell_factors(mat[side, z], pml[side, z], table)
        source = [s[side, c, z].astype(jnp.float32) for c in range(3)]
        incoming = [e[side, c, z] + source[c] for c in range(3)]
        v = [drive * f for f in incoming]
        q = [decay * f + g for f, g in zip(incoming, source)]
        return v, q, drive, [h[side, c, z] for c in range(3)]

    v, q, drive, mag = layer(1, 1)
    w, _, _, deep = layer(1, 0)
    deep_x = deep[0] + (next_y(w[2]) - (v[1] - w[1]))
    deep_y = deep[1] + ((v[0] - w[0]) - next_x(w[2]))
    low = [
        mag[0] + (next_y(v[2]) + v[1]),
        mag[1] - (v[0] + next_x(v[2])),
        mag[2] + (next_x(v[1]) - next_y(v[0])),
        q[0] - DT_STEP * deep_y,
        q[1] + DT_STEP * deep_x,
        q[2],
        drive,
        jnp.where(row == 0, v[1][:1], jnp.where(row == 1, v[2][:1], w[2][:1])),
    ]
    v, q, drive, mag = layer(0, 0)
    w, _, _, _ = layer(0, 1)
    edge_x = mag[0] + (next_y(v[2]) - (w[1] - v[1]))
    edge_y = mag[1] + (w[0] - v[0])
    high = [v[0], v[1], v[2], q[0], q[1] - DT_STEP * edge_x, drive, edge_y, mag[2]]

    def put(top, bottom):
        for slot in range(Z_SLOTS):
            top[pl.ds(slot * nx, nx), :] = low[slot]
            bottom[pl.ds(slot * nx, nx), :] = high[slot]

    either(is_odd("gz"), put, za, zb)


def prepare_kernel(nz, nx, eps_in, e_in, h_in, s_in, mat_in, pml_in, work, eps, *rest):
    bufs, sems = rest[:-1], rest[-1]
    copies = [
        pltpu.make_async_copy(source, target, sems.at[k])
        for k, (source, target) in enumerate(
            zip((eps_in, mat_in, pml_in, s_in, e_in, h_in), (eps,) + bufs)
        )
    ]
    for copy in copies:
        copy.start()
    mat, pml, s, e, h = bufs
    for copy in copies[:5]:
        copy.wait()
    table = inverse_table(eps, nx)
    tall = nx * (nz + 2)
    for z in range(nz):
        decay, drive, inv = cell_factors(mat[z], pml[z], table)

        def keep(field, value):
            work[pl.ds(field * tall + (z + 1) * nx, nx), :] = value

        keep(DR, drive)
        keep(DECAY, decay)
        keep(INV, inv)
        for c in range(3):
            source = s[c, z].astype(jnp.float32)
            incoming = e[c, z] + source
            keep(V0 + c, drive * incoming)
            keep(Q0 + c, decay * incoming + source)
            keep(I0 + c, incoming)
    copies[5].wait()
    for c in range(3):
        for z in range(nz):
            work[pl.ds((H0 + c) * tall + (z + 1) * nx, nx), :] = h[c, z]


def columns_kernel(nz, nx, za, zb, work, zh, xa, xb):
    tall = nx * (nz + 2)
    deep = nz + 2
    zero = jnp.zeros((nx, 128), jnp.float32)

    def take(low, high):
        for field in range(V0, H2 + 1):
            for k, (slots, ref) in enumerate(((Z_LOW, low), (Z_HIGH, high))):
                at = pl.ds((2 * field + k) * nx, nx)
                if field in slots:
                    zh[at, :] = ref[pl.ds(slots.index(field) * nx, nx), :]
                else:
                    zh[at, :] = zero

    odd_z = is_odd("gz")
    either(odd_z, take, zb, za)
    index = jnp.where(odd_z, 0, 1)
    row, first, last = masks(deep)

    def extra(k):
        at = pl.ds(EXTRA_Z * nx + k, 1)
        return jnp.where(jnp.broadcast_to(index, (1, 128)) == 0, za[at, :], zb[at, :])

    for k in range(2):
        zh[pl.ds(20 * nx + k, 1), :] = extra(k)

    def next_y(f):
        return jnp.where(last, 0.0, pltpu.roll(f, 127, 1)) - f

    def prev_y(f):
        return f - jnp.where(first, 0.0, pltpu.roll(f, 1, 1))

    def next_z(f):
        return jnp.where(row == deep - 1, 0.0, pltpu.roll(f, deep - 1, 0) - f)

    def prev_z(f):
        return f - jnp.where(row == 0, 0.0, pltpu.roll(f, 1, 0))

    def column(field, x):
        own = work[pl.ds(field * tall + x, deep, stride=nx), :]
        below, above = (zh[pl.ds((2 * field + k) * nx + x, 1), :] for k in range(2))
        return jnp.where(row == 0, below, jnp.where(row == deep - 1, above, own))

    bottom_edge = jnp.logical_and(row == 0, jnp.broadcast_to(lax.axis_index("gz"), row.shape) == 0)

    x = nx - 1
    v = [column(V0 + c, x) for c in range(3)]
    w = [column(V0 + c, x - 1) for c in range(3)]
    mag_x = column(H0, x) + (next_y(v[2]) - next_z(v[1]))
    mag_x = jnp.where(bottom_edge, 0.0, mag_x)
    deep_y = column(H1, x - 1) + (next_z(w[0]) - (v[2] - w[2]))
    deep_z = column(H2, x - 1) + ((v[1] - w[1]) - next_y(w[0]))
    low = [
        column(H1, x) + (next_z(v[0]) + v[2]),
        column(H2, x) - (v[1] + next_y(v[0])),
        column(Q0, x),
        column(Q1, x) - DT_STEP * (prev_z(mag_x) + deep_z),
        column(Q2, x) + DT_STEP * (deep_y + prev_y(mag_x)),
        column(DR, x),
    ]

    v = [column(V0 + c, 0) for c in range(3)]
    w = [column(V0 + c, 1) for c in range(3)]
    mag_x = column(H0, 0) + (next_y(v[2]) - next_z(v[1]))
    mag_x = jnp.where(bottom_edge, 0.0, mag_x)
    mag_y = column(H1, 0) + (next_z(v[0]) - (w[2] - v[2]))
    mag_z = column(H2, 0) + ((w[1] - v[1]) - next_y(v[0]))
    high = [
        jnp.where(row == 0, extra(0), v[1]),
        jnp.where(row == 0, extra(1), v[2]),
        column(Q1, 0) - DT_STEP * (prev_z(mag_x) - mag_z),
        column(Q2, 0) - DT_STEP * (mag_y - prev_y(mag_x)),
        column(DR, 0),
        jnp.broadcast_to(extra(2), (deep, 128)),
    ]

    def put(top, bottom):
        for slot in range(X_SLOTS):
            top[pl.ds(slot * deep, deep), :] = low[slot]
            bottom[pl.ds(slot * deep, deep), :] = high[slot]

    either(is_odd("xy"), put, xa, xb)


def weight_kernel(nz, nx, saved, work, weight, column):
    cells, tall = nz * nx, nx * (nz + 2)
    total = jnp.zeros((nx, 128), jnp.float32)
    for z in range(nz):
        near = pl.ds(DECAY * tall + (z + 1) * nx, nx)
        decay = work[near, :]
        inv = work[pl.ds(INV * tall + (z + 1) * nx, nx), :]
        cell = jnp.zeros((nx, 128), jnp.float32)
        for c in range(3):
            times = [
                saved[pl.ds((3 * t + c) * cells + z * nx, nx), :].astype(jnp.float32)
                for t in range(3)
            ]
            incoming = work[pl.ds((I0 + c) * tall + (z + 1) * nx, nx), :]
            cell = cell + incoming * (times[2] - decay * times[1])
            weight[pl.ds(c * cells + z * nx, nx), :] = (times[1] - decay * times[0]) * inv
        total = total + cell * inv
    column[...] = total


def march_kernel(
    nz, nx, layers, work, zh, weight, column, xa, xb, blocks, e_out, h_out, sums, xh, out_e, out_h, sems
):
    cells, tall, deep = nz * nx, nx * (nz + 2), nz + 2
    index_z, index_x = lax.axis_index("gz"), lax.axis_index("xy")
    odd_x = is_odd("xy")
    xh[...] = jnp.zeros_like(xh)

    def take(low, high):
        for slots, ref, place in ((X_LOW, low, 7), (X_HIGH, high, 0)):
            for slot, field in enumerate(slots):
                at = pl.ds(field * deep * 8 + place, deep, stride=8)
                xh[at, :] = ref[pl.ds(slot * deep, deep), :]

    either(odd_x, take, xb, xa)
    at = pl.ds(EXTRA_X * deep, 1)
    beyond = jnp.where(jnp.broadcast_to(odd_x, (1, 128)), xb[at, :], xa[at, :])

    rows = nx + 8
    row, first, last = masks(rows)
    inside_x = jnp.logical_or(
        row < nx, jnp.logical_and(row == rows - 1, jnp.broadcast_to(index_x, row.shape) > 0)
    )
    inside_z = jnp.logical_and(inside_x, jnp.broadcast_to(index_z, row.shape) > 0)

    def load(field, z):
        if 0 <= z < nz:
            own = work[pl.ds(field * tall + (z + 1) * nx, nx), :]
        else:
            own = zh[pl.ds((2 * field + (z > 0)) * nx, nx), :]
        side = xh[pl.ds((field * deep + z + 1) * 8, 8), :]
        return jnp.concatenate([own, side], axis=0)

    def next_y(f):
        return jnp.where(last, 0.0, pltpu.roll(f, 127, 1)) - f

    def prev_y(f):
        return f - jnp.where(first, 0.0, pltpu.roll(f, 1, 1))

    def next_x(f):
        return pltpu.roll(f, rows - 1, 0) - f

    def prev_x(f):
        return f - pltpu.roll(f, 1, 0)

    def magnetic(z, old, here, above):
        keep = inside_z if z < 0 else inside_x
        out = [
            old[0] + (next_y(here[2]) - (above[1] - here[1])),
            old[1] + ((above[0] - here[0]) - next_x(here[2])),
            old[2] + (next_x(here[1]) - next_y(here[0])),
        ]
        return [jnp.where(keep, f, 0.0) for f in out]

    def curl_p(here, below):
        return [
            prev_y(here[2]) - (here[1] - below[1]),
            (here[0] - below[0]) - prev_x(here[2]),
            prev_x(here[1]) - prev_y(here[0]),
        ]

    def flush(z):
        for c in range(3):
            at = pl.ds(c * cells + z * nx, nx * 2)
            for k, (source, target) in enumerate(((out_e, e_out), (out_h, h_out))):
                sem = sems.at[k * 3 + c]
                pltpu.make_async_copy(source.at[at, :], target.at[at, :], sem).start()

    zeros = jnp.zeros((rows, 128), jnp.float32)
    total = column[...]
    v_here = [load(V0 + c, -1) for c in range(3)]
    mag_below = [zeros] * 3
    mag_mid = mag2_below = inc_below = drv_below = None
    for z in range(-1, nz + 1):
        v_above = [load(V0 + c, z + 1) for c in range(3)] if z < nz else v_here
        old = [load(H0 + c, z) for c in range(3)]
        if z < 0:
            side_y, side_z = (zh[pl.ds(20 * nx + k, 1), :] for k in range(2))
            old[1] = old[1] - jnp.where(row == rows - 1, side_z, 0.0)
            old[2] = old[2] + jnp.where(row == rows - 1, side_y, 0.0)
        mag = magnetic(z, old, v_here, v_above)
        if z == nz:
            mag[0] = zeros
        v_here = v_above
        curl = curl_p(mag, mag_below)
        inc = [load(Q0 + c, z) - DT_STEP * curl[c] for c in range(3)]
        if z < 0:
            inc[0] = inc[0] + jnp.where(row == nx - 1, DT_STEP * beyond, 0.0)
        drive = load(DR, z)
        drv = [drive * f for f in inc]
        if 0 <= z < nz:
            cell = jnp.zeros((nx, 128), jnp.float32)
            for c in range(3):
                cell = cell + inc[c][:nx] * weight[pl.ds(c * cells + z * nx, nx), :]
            total = total + cell
        if z >= 0:
            low = z - 1
            mag2 = magnetic(low, mag_mid, drv_below, drv)
            if low >= 0:
                decay = work[pl.ds(DECAY * tall + (low + 1) * nx, nx), :]
                curl = curl_p(mag2, mag2_below)
                for c in range(3):
                    at = pl.ds(c * cells + low * nx, nx)
                    out_h[at, :] = mag2[c][:nx]
                    out_e[at, :] = decay * inc_below[c][:nx] - DT_STEP * curl[c][:nx]
                if low % 2 == 1:
                    flush(low - 1)
            mag2_below = mag2
        inc_below, drv_below = inc, drv
        mag_mid, mag_below = mag, mag

    devices = sums.shape[0]
    total = total * (-1.0 / layers)
    owner = B_DEV * lax.broadcasted_iota(jnp.int32, (devices, 128), 0)
    spot = lax.broadcasted_iota(jnp.int32, (devices, 128), 1)
    parts = [jnp.zeros((devices, 128), jnp.float32) for _ in range(B_DEV)]
    for group in range(nx // 4):
        four = jnp.sum(total[4 * group : 4 * group + 4], axis=0, keepdims=True)
        label = blocks[pl.ds(4 * group, 1), :]
        for k in range(B_DEV):
            parts[k] = parts[k] + jnp.where(label == owner + k, four, 0.0)
    packed = jnp.zeros((devices, 128), jnp.float32)
    for k in range(B_DEV):
        packed = jnp.where(spot == k, jnp.sum(parts[k], axis=1, keepdims=True), packed)
    sums[...] = packed

    for c in range(3):
        at = pl.ds(c * cells, cells)
        for k, (source, target) in enumerate(((out_e, e_out), (out_h, h_out))):
            pltpu.make_async_copy(source.at[at, :], target.at[at, :], sems.at[k * 3 + c]).wait()


def swap_pairs(count, offset):
    pairs = []
    for low in range(offset, count - 1, 2):
        pairs += [(low, low + 1), (low + 1, low)]
    return pairs


def estimate(flops, moved):
    return pl.CostEstimate(flops=flops, bytes_accessed=moved, transcendentals=0)


def on_device(
    adjoint_e, adjoint_h, source_e, e_saved, material_eps, material_id, pml_level, block_map
):
    nz, nx, ny = material_id.shape
    slabs, tiles = lax.axis_size("gz"), lax.axis_size("xy")
    cells, tall, deep = nz * nx, nx * (nz + 2), nz + 2
    field = cells * ny
    f32, bf16, i32 = jnp.float32, jnp.bfloat16, jnp.int32
    params = pltpu.CompilerParams(vmem_limit_bytes=24 * 1024 * 1024)
    raw = (material_eps, adjoint_e, adjoint_h, source_e, material_id, pml_level)
    raw = [pltpu.with_memory_space_constraint(a, pltpu.HBM) for a in raw]
    table = pltpu.SMEM(material_eps.shape, f32)
    z_msg, x_msg = shape_of(Z_SLOTS * nx, ny), shape_of(X_SLOTS * deep, ny)

    za, zb = pl.pallas_call(
        functools.partial(faces_kernel, nz, nx),
        out_shape=(z_msg, z_msg),
        in_specs=[HBM] * 6,
        out_specs=(VMEM,) * 2,
        scratch_shapes=[
            table,
            pltpu.VMEM((2, 3, 2, nx, ny), f32),
            pltpu.VMEM((2, 3, 2, nx, ny), f32),
            pltpu.VMEM((2, 3, 2, nx, ny), bf16),
            pltpu.VMEM((2, 2, nx, ny), i32),
            pltpu.VMEM((2, 2, nx, ny), i32),
            pltpu.SemaphoreType.DMA((11,)),
        ],
        compiler_params=params,
        cost_estimate=estimate(60 * field // 4, 4 * 4 * field),
        name="faces",
    )(*raw)

    za = lax.ppermute(za, "gz", swap_pairs(slabs, 0))
    zb = lax.ppermute(zb, "gz", swap_pairs(slabs, 1))

    work = pl.pallas_call(
        functools.partial(prepare_kernel, nz, nx),
        out_shape=shape_of(FIELDS * tall, ny),
        in_specs=[HBM] * 6,
        out_specs=VMEM,
        scratch_shapes=[
            table,
            pltpu.VMEM((nz, nx, ny), i32),
            pltpu.VMEM((nz, nx, ny), i32),
            pltpu.VMEM((3, nz, nx, ny), bf16),
            pltpu.VMEM((3, nz, nx, ny), f32),
            pltpu.VMEM((3, nz, nx, ny), f32),
            pltpu.SemaphoreType.DMA((6,)),
        ],
        compiler_params=params,
        cost_estimate=estimate(80 * field, 4 * 25 * field),
        name="prepare",
    )(*raw)

    zh, xa, xb = pl.pallas_call(
        functools.partial(columns_kernel, nz, nx),
        out_shape=(shape_of(20 * nx + 8, ny), x_msg, x_msg),
        in_specs=[VMEM] * 3,
        out_specs=(VMEM,) * 3,
        compiler_params=params,
        cost_estimate=estimate(4 * field, 4 * field),
        name="columns",
    )(za, zb, work)

    xa = lax.ppermute(xa, "xy", swap_pairs(tiles, 0))
    xb = lax.ppermute(xb, "xy", swap_pairs(tiles, 1))

    weight, column = pl.pallas_call(
        functools.partial(weight_kernel, nz, nx),
        out_shape=(shape_of(3 * cells, ny), shape_of(nx, ny)),
        in_specs=[VMEM] * 2,
        out_specs=(VMEM,) * 2,
        compiler_params=params,
        cost_estimate=estimate(40 * field, 4 * 12 * field),
        name="weights",
    )(e_saved.reshape(-1, ny), work)

    field_e, field_h, sums = pl.pallas_call(
        functools.partial(march_kernel, nz, nx, nz * slabs),
        out_shape=(shape_of(3 * cells, ny), shape_of(3 * cells, ny), shape_of(slabs * tiles, ny)),
        in_specs=[VMEM] * 7,
        out_specs=(HBM, HBM, VMEM),
        scratch_shapes=[
            pltpu.VMEM((10 * deep * 8, ny), f32),
            pltpu.VMEM((3 * cells, ny), f32),
            pltpu.VMEM((3 * cells, ny), f32),
            pltpu.SemaphoreType.DMA((6,)),
        ],
        compiler_params=params,
        cost_estimate=estimate(200 * field, 4 * 25 * field),
        name="march",
    )(work, zh, weight, column, xa, xb, block_map)

    gathered = lax.all_to_all(sums, ("gz", "xy"), 0, 0, tiled=True)
    design_grad = jnp.sum(gathered, axis=0)[:B_DEV]
    return field_e.reshape(adjoint_e.shape), field_h.reshape(adjoint_h.shape), design_grad


def solution(mesh):
    placed = (
        P(None, "gz", "xy", None),
        P(None, "gz", "xy", None),
        P(None, "gz", "xy", None),
        P(None, None, "gz", "xy", None),
        P(),
        P("gz", "xy", None),
        P("gz", "xy", None),
        P("xy", None),
    )
    return jax.shard_map(
        on_device,
        mesh=mesh,
        in_specs=placed,
        out_specs=(P(None, "gz", "xy", None), P(None, "gz", "xy", None), P(("gz", "xy"))),
        check_vma=False,
    )
```

```python
import functools

import jax
import jax.numpy as jnp
from jax import lax
from jax.experimental import pallas as pl
from jax.experimental.pallas import tpu as pltpu
from jax.sharding import PartitionSpec as P

B_DEV = 2

DT_STEP = 0.5
SIGMA_UNIT = 0.15

V0, V1, V2, Q0, Q1, Q2, DR, H0, H1, H2, I0, I1, I2, DECAY, INV = range(15)
FIELDS = 15

Z_LOW = (H0, H1, H2, Q0, Q1, Q2, DR)
Z_HIGH = (V0, V1, V2, Q0, Q1, DR, H1, H2)
X_LOW = (H1, H2, Q0, Q1, Q2, DR)
X_HIGH = (V1, V2, Q1, Q2, DR)
EXTRA_Z = 7
EXTRA_X = 5
Z_SLOTS, X_SLOTS = 8, 6

VMEM = pl.BlockSpec(memory_space=pltpu.VMEM)
HBM = pl.BlockSpec(memory_space=pltpu.HBM)


def shape_of(rows, ny):
    return jax.ShapeDtypeStruct((rows, ny), jnp.float32)


def is_odd(axis):
    return lax.rem(lax.axis_index(axis), 2) == 1


def either(odd, body, first, second):
    pl.when(jnp.logical_not(odd))(functools.partial(body, first, second))
    pl.when(odd)(functools.partial(body, second, first))


def masks(tall):
    row = lax.broadcasted_iota(jnp.int32, (tall, 128), 0)
    lane = lax.broadcasted_iota(jnp.int32, (tall, 128), 1)
    return row, lane == 0, lane == 127


def inverse_table(eps, nx):
    return [1.0 / jnp.full((nx, 128), eps[k], jnp.float32) for k in range(eps.shape[0])]


def cell_factors(kind, level, table):
    inv = table[0]
    for k in range(1, len(table)):
        inv = jnp.where(kind == k, table[k], inv)
    sigma = SIGMA_UNIT * level.astype(jnp.float32)
    recip = 1.0 / (1.0 + sigma)
    return (1.0 - sigma) * recip, DT_STEP * inv * recip, inv


def faces_kernel(nz, nx, eps_in, e_in, h_in, s_in, mat_in, pml_in, zb, za, eps, *rest):
    bufs, sems = rest[:-1], rest[-1]
    copies = [pltpu.make_async_copy(eps_in, eps, sems.at[0])]
    for k, ref in enumerate((e_in, h_in, s_in, mat_in, pml_in)):
        for side, start in enumerate((0, nz - 2)):
            part = pl.ds(start, 2)
            source = ref.at[:, part] if k < 3 else ref.at[part]
            copies.append(pltpu.make_async_copy(source, bufs[k].at[side], sems.at[len(copies)]))
    for copy in copies:
        copy.start()
    for copy in copies:
        copy.wait()
    e, h, s, mat, pml = bufs
    table = inverse_table(eps, nx)
    row, first, last = masks(nx)

    def next_y(f):
        return jnp.where(last, 0.0, pltpu.roll(f, 127, 1)) - f

    def next_x(f):
        return jnp.where(row == nx - 1, 0.0, pltpu.roll(f, nx - 1, 0)) - f

    def layer(side, z):
        decay, drive, _ = cell_factors(mat[side, z], pml[side, z], table)
        source = [s[side, c, z].astype(jnp.float32) for c in range(3)]
        incoming = [e[side, c, z] + source[c] for c in range(3)]
        v = [drive * f for f in incoming]
        q = [decay * f + g for f, g in zip(incoming, source)]
        return v, q, drive, [h[side, c, z] for c in range(3)]

    v, q, drive, mag = layer(1, 1)
    w, _, _, deep = layer(1, 0)
    deep_x = deep[0] + (next_y(w[2]) - (v[1] - w[1]))
    deep_y = deep[1] + ((v[0] - w[0]) - next_x(w[2]))
    low = [
        mag[0] + (next_y(v[2]) + v[1]),
        mag[1] - (v[0] + next_x(v[2])),
        mag[2] + (next_x(v[1]) - next_y(v[0])),
        q[0] - DT_STEP * deep_y,
        q[1] + DT_STEP * deep_x,
        q[2],
        drive,
        jnp.where(row == 0, v[1][:1], jnp.where(row == 1, v[2][:1], w[2][:1])),
    ]
    v, q, drive, mag = layer(0, 0)
    w, _, _, _ = layer(0, 1)
    edge_x = mag[0] + (next_y(v[2]) - (w[1] - v[1]))
    edge_y = mag[1] + (w[0] - v[0])
    high = [v[0], v[1], v[2], q[0], q[1] - DT_STEP * edge_x, drive, edge_y, mag[2]]

    def put(top, bottom):
        for slot in range(Z_SLOTS):
            top[pl.ds(slot * nx, nx), :] = low[slot]
            bottom[pl.ds(slot * nx, nx), :] = high[slot]

    either(is_odd("gz"), put, za, zb)


def prepare_kernel(nz, nx, eps_in, e_in, h_in, s_in, mat_in, pml_in, work, eps, *rest):
    bufs, sems = rest[:-1], rest[-1]
    copies = [
        pltpu.make_async_copy(source, target, sems.at[k])
        for k, (source, target) in enumerate(
            zip((eps_in, mat_in, pml_in, s_in, e_in, h_in), (eps,) + bufs)
        )
    ]
    for copy in copies:
        copy.start()
    mat, pml, s, e, h = bufs
    for copy in copies[:5]:
        copy.wait()
    table = inverse_table(eps, nx)
    tall = nx * (nz + 2)
    for z in range(nz):
        decay, drive, inv = cell_factors(mat[z], pml[z], table)

        def keep(field, value):
            work[pl.ds(field * tall + (z + 1) * nx, nx), :] = value

        keep(DR, drive)
        keep(DECAY, decay)
        keep(INV, inv)
        for c in range(3):
            source = s[c, z].astype(jnp.float32)
            incoming = e[c, z] + source
            keep(V0 + c, drive * incoming)
            keep(Q0 + c, decay * incoming + source)
            keep(I0 + c, incoming)
    copies[5].wait()
    for c in range(3):
        for z in range(nz):
            work[pl.ds((H0 + c) * tall + (z + 1) * nx, nx), :] = h[c, z]


def columns_kernel(nz, nx, zb, za, work, zh, xb, xa):
    tall = nx * (nz + 2)
    deep = nz + 2
    zero = jnp.zeros((nx, 128), jnp.float32)

    def take(low, high):
        for field in range(V0, H2 + 1):
            for k, (slots, ref) in enumerate(((Z_LOW, low), (Z_HIGH, high))):
                at = pl.ds((2 * field + k) * nx, nx)
                if field in slots:
                    zh[at, :] = ref[pl.ds(slots.index(field) * nx, nx), :]
                else:
                    zh[at, :] = zero

    odd_z = is_odd("gz")
    either(odd_z, take, zb, za)
    index = jnp.where(odd_z, 0, 1)
    row, first, last = masks(deep)

    def extra(k):
        at = pl.ds(EXTRA_Z * nx + k, 1)
        return jnp.where(jnp.broadcast_to(index, (1, 128)) == 0, za[at, :], zb[at, :])

    for k in range(2):
        zh[pl.ds(20 * nx + k, 1), :] = extra(k)

    def next_y(f):
        return jnp.where(last, 0.0, pltpu.roll(f, 127, 1)) - f

    def prev_y(f):
        return f - jnp.where(first, 0.0, pltpu.roll(f, 1, 1))

    def next_z(f):
        return jnp.where(row == deep - 1, 0.0, pltpu.roll(f, deep - 1, 0) - f)

    def prev_z(f):
        return f - jnp.where(row == 0, 0.0, pltpu.roll(f, 1, 0))

    def column(field, x):
        own = work[pl.ds(field * tall + x, deep, stride=nx), :]
        below, above = (zh[pl.ds((2 * field + k) * nx + x, 1), :] for k in range(2))
        return jnp.where(row == 0, below, jnp.where(row == deep - 1, above, own))

    bottom_edge = jnp.logical_and(row == 0, jnp.broadcast_to(lax.axis_index("gz"), row.shape) == 0)

    x = nx - 1
    v = [column(V0 + c, x) for c in range(3)]
    w = [column(V0 + c, x - 1) for c in range(3)]
    mag_x = column(H0, x) + (next_y(v[2]) - next_z(v[1]))
    mag_x = jnp.where(bottom_edge, 0.0, mag_x)
    deep_y = column(H1, x - 1) + (next_z(w[0]) - (v[2] - w[2]))
    deep_z = column(H2, x - 1) + ((v[1] - w[1]) - next_y(w[0]))
    low = [
        column(H1, x) + (next_z(v[0]) + v[2]),
        column(H2, x) - (v[1] + next_y(v[0])),
        column(Q0, x),
        column(Q1, x) - DT_STEP * (prev_z(mag_x) + deep_z),
        column(Q2, x) + DT_STEP * (deep_y + prev_y(mag_x)),
        column(DR, x),
    ]

    v = [column(V0 + c, 0) for c in range(3)]
    w = [column(V0 + c, 1) for c in range(3)]
    mag_x = column(H0, 0) + (next_y(v[2]) - next_z(v[1]))
    mag_x = jnp.where(bottom_edge, 0.0, mag_x)
    mag_y = column(H1, 0) + (next_z(v[0]) - (w[2] - v[2]))
    mag_z = column(H2, 0) + ((w[1] - v[1]) - next_y(v[0]))
    high = [
        jnp.where(row == 0, extra(0), v[1]),
        jnp.where(row == 0, extra(1), v[2]),
        column(Q1, 0) - DT_STEP * (prev_z(mag_x) - mag_z),
        column(Q2, 0) - DT_STEP * (mag_y - prev_y(mag_x)),
        column(DR, 0),
        jnp.broadcast_to(extra(2), (deep, 128)),
    ]

    def put(top, bottom):
        for slot in range(X_SLOTS):
            top[pl.ds(slot * deep, deep), :] = low[slot]
            bottom[pl.ds(slot * deep, deep), :] = high[slot]

    either(is_odd("xy"), put, xa, xb)


def spread(fours, groups, blocks, shape):
    owner = lax.broadcasted_iota(jnp.int32, shape, 0)
    out = jnp.zeros(shape, jnp.float32)
    for four, group in zip(fours, groups):
        out = out + jnp.where(blocks[pl.ds(4 * group, 1), :] == owner, four, 0.0)
    return out


def interior_kernel(nz, nx, layers, saved, work, zh, blocks, partial, edges, weight):
    cells, tall = nz * nx, nx * (nz + 2)
    row, first, last = masks(nx)
    above_edge = jnp.broadcast_to(lax.axis_index("gz"), row.shape) > 0

    def load(field, z):
        if 0 <= z < nz:
            return work[pl.ds(field * tall + (z + 1) * nx, nx), :]
        return zh[pl.ds((2 * field + (z > 0)) * nx, nx), :]

    def next_y(f):
        return jnp.where(last, 0.0, pltpu.roll(f, 127, 1)) - f

    def prev_y(f):
        return f - jnp.where(first, 0.0, pltpu.roll(f, 1, 1))

    def next_x(f):
        return jnp.where(row == nx - 1, 0.0, pltpu.roll(f, nx - 1, 0)) - f

    def prev_x(f):
        return f - jnp.where(row == 0, 0.0, pltpu.roll(f, 1, 0))

    total = jnp.zeros((nx, 128), jnp.float32)
    here = [load(V0 + c, -1) for c in range(3)]
    below = None
    for z in range(-1, nz):
        above = [load(V0 + c, z + 1) for c in range(3)]
        mag = [
            load(H0, z) + (next_y(here[2]) - (above[1] - here[1])),
            load(H1, z) + ((above[0] - here[0]) - next_x(here[2])),
        ]
        if z < 0:
            mag = [jnp.where(above_edge, f, 0.0) for f in mag]
        else:
            mag.append(load(H2, z) + (next_x(here[1]) - next_y(here[0])))
            curl = [
                prev_y(mag[2]) - (mag[1] - below[1]),
                (mag[0] - below[0]) - prev_x(mag[2]),
                prev_x(mag[1]) - prev_y(mag[0]),
            ]
            decay, inv = load(DECAY, z), load(INV, z)
            cell = jnp.zeros((nx, 128), jnp.float32)
            for c in range(3):
                times = [
                    saved[pl.ds((3 * t + c) * cells + z * nx, nx), :].astype(jnp.float32)
                    for t in range(3)
                ]
                factor = times[1] - decay * times[0]
                weight[pl.ds(c * tall + (z + 1) * nx, nx), :] = factor * inv
                cell = cell + load(I0 + c, z) * (times[2] - decay * times[1])
                cell = cell + (load(Q0 + c, z) - DT_STEP * curl[c]) * factor
            total = total + cell * inv
        here, below = above, mag
    total = total * (-1.0 / layers)
    fours = [
        jnp.sum(total[4 * k : 4 * k + 4], axis=0, keepdims=True) for k in range(nx // 4)
    ]
    partial[...] = spread(fours, range(nx // 4), blocks, partial.shape)
    for side, x in enumerate((0, nx - 1)):
        for c in range(3):
            part = weight[pl.ds(c * tall + nx + x, nz, stride=nx), :]
            edges[pl.ds((3 * side + c) * (nz + 2) + 1, nz), :] = part


def edge_kernel(nz, nx, layers, work, partial, edges, blocks, xb, xa, sums):
    tall, deep = nx * (nz + 2), nz + 2
    row, first, last = masks(deep)
    odd_x = jnp.broadcast_to(is_odd("xy"), row.shape)
    own = jnp.logical_and(row > 0, row < deep - 1)
    low_side = jnp.logical_and(own, jnp.broadcast_to(lax.axis_index("xy"), row.shape) > 0)

    def slot(slots, field):
        at = pl.ds(slots.index(field) * deep, deep)
        return jnp.where(odd_x, xa[at, :], xb[at, :]), jnp.where(odd_x, xb[at, :], xa[at, :])

    def prev_y(f):
        return f - jnp.where(first, 0.0, pltpu.roll(f, 1, 1))

    def factor(side, c):
        return edges[pl.ds((3 * side + c) * deep, deep), :]

    mag_y = slot(X_LOW, H1)[0] - work[pl.ds(V2 * tall, deep, stride=nx), :]
    mag_z = slot(X_LOW, H2)[0] + work[pl.ds(V1 * tall, deep, stride=nx), :]
    near = DT_STEP * (mag_y * factor(0, 2) - mag_z * factor(0, 1))
    v_y, v_z = slot(X_HIGH, V1)[1], slot(X_HIGH, V2)[1]
    far = DT_STEP * (
        v_y * factor(1, 1)
        + v_z * factor(1, 2)
        - (prev_y(v_y) + (v_z - pltpu.roll(v_z, 1, 0))) * factor(1, 0)
    )
    near = jnp.sum(jnp.where(low_side, near, 0.0), axis=0, keepdims=True)
    far = jnp.sum(jnp.where(own, far, 0.0), axis=0, keepdims=True)

    ends = (near * (-1.0 / layers), far * (-1.0 / layers))
    sums[...] = partial[...] + spread(ends, (0, nx // 4 - 1), blocks, sums.shape)


def march_kernel(
    nz, nx, work, zh, xb, xa, e_out, h_out, xh, out_e, out_h, sems
):
    cells, tall, deep = nz * nx, nx * (nz + 2), nz + 2
    index_z, index_x = lax.axis_index("gz"), lax.axis_index("xy")
    odd_x = is_odd("xy")
    xh[...] = jnp.zeros_like(xh)

    def take(low, high):
        for slots, ref, place in ((X_LOW, low, 7), (X_HIGH, high, 0)):
            for slot, field in enumerate(slots):
                at = pl.ds(field * deep * 8 + place, deep, stride=8)
                xh[at, :] = ref[pl.ds(slot * deep, deep), :]

    either(odd_x, take, xb, xa)
    at = pl.ds(EXTRA_X * deep, 1)
    beyond = jnp.where(jnp.broadcast_to(odd_x, (1, 128)), xb[at, :], xa[at, :])

    rows = nx + 8
    row, first, last = masks(rows)
    inside_x = jnp.logical_or(
        row < nx, jnp.logical_and(row == rows - 1, jnp.broadcast_to(index_x, row.shape) > 0)
    )
    inside_z = jnp.logical_and(inside_x, jnp.broadcast_to(index_z, row.shape) > 0)

    def load(field, z):
        if 0 <= z < nz:
            own = work[pl.ds(field * tall + (z + 1) * nx, nx), :]
        else:
            own = zh[pl.ds((2 * field + (z > 0)) * nx, nx), :]
        side = xh[pl.ds((field * deep + z + 1) * 8, 8), :]
        return jnp.concatenate([own, side], axis=0)

    def next_y(f):
        return jnp.where(last, 0.0, pltpu.roll(f, 127, 1)) - f

    def prev_y(f):
        return f - jnp.where(first, 0.0, pltpu.roll(f, 1, 1))

    def next_x(f):
        return pltpu.roll(f, rows - 1, 0) - f

    def prev_x(f):
        return f - pltpu.roll(f, 1, 0)

    def magnetic(z, old, here, above):
        keep = inside_z if z < 0 else inside_x
        out = [
            old[0] + (next_y(here[2]) - (above[1] - here[1])),
            old[1] + ((above[0] - here[0]) - next_x(here[2])),
            old[2] + (next_x(here[1]) - next_y(here[0])),
        ]
        return [jnp.where(keep, f, 0.0) for f in out]

    def curl_p(here, below):
        return [
            prev_y(here[2]) - (here[1] - below[1]),
            (here[0] - below[0]) - prev_x(here[2]),
            prev_x(here[1]) - prev_y(here[0]),
        ]

    def flush(z):
        for c in range(3):
            at = pl.ds(c * cells + z * nx, nx * 2)
            for k, (source, target) in enumerate(((out_e, e_out), (out_h, h_out))):
                sem = sems.at[k * 3 + c]
                pltpu.make_async_copy(source.at[at, :], target.at[at, :], sem).start()

    zeros = jnp.zeros((rows, 128), jnp.float32)
    v_here = [load(V0 + c, -1) for c in range(3)]
    mag_below = [zeros] * 3
    mag_mid = mag2_below = inc_below = drv_below = None
    for z in range(-1, nz + 1):
        v_above = [load(V0 + c, z + 1) for c in range(3)] if z < nz else v_here
        old = [load(H0 + c, z) for c in range(3)]
        if z < 0:
            side_y, side_z = (zh[pl.ds(20 * nx + k, 1), :] for k in range(2))
            old[1] = old[1] - jnp.where(row == rows - 1, side_z, 0.0)
            old[2] = old[2] + jnp.where(row == rows - 1, side_y, 0.0)
        mag = magnetic(z, old, v_here, v_above)
        if z == nz:
            mag[0] = zeros
        v_here = v_above
        curl = curl_p(mag, mag_below)
        inc = [load(Q0 + c, z) - DT_STEP * curl[c] for c in range(3)]
        if z < 0:
            inc[0] = inc[0] + jnp.where(row == nx - 1, DT_STEP * beyond, 0.0)
        drive = load(DR, z)
        drv = [drive * f for f in inc]
        if z >= 0:
            low = z - 1
            mag2 = magnetic(low, mag_mid, drv_below, drv)
            if low >= 0:
                decay = work[pl.ds(DECAY * tall + (low + 1) * nx, nx), :]
                curl = curl_p(mag2, mag2_below)
                for c in range(3):
                    at = pl.ds(c * cells + low * nx, nx)
                    out_h[at, :] = mag2[c][:nx]
                    out_e[at, :] = decay * inc_below[c][:nx] - DT_STEP * curl[c][:nx]
                if low % 2 == 1:
                    flush(low - 1)
            mag2_below = mag2
        inc_below, drv_below = inc, drv
        mag_mid, mag_below = mag, mag

    for c in range(3):
        at = pl.ds(c * cells, cells)
        for k, (source, target) in enumerate(((out_e, e_out), (out_h, h_out))):
            pltpu.make_async_copy(source.at[at, :], target.at[at, :], sems.at[k * 3 + c]).wait()


def swap_pairs(count, offset):
    pairs = []
    for low in range(offset, count - 1, 2):
        pairs += [(low, low + 1), (low + 1, low)]
    return pairs


def estimate(flops, moved):
    return pl.CostEstimate(flops=flops, bytes_accessed=moved, transcendentals=0)


def on_device(
    adjoint_e, adjoint_h, source_e, e_saved, material_eps, material_id, pml_level, block_map
):
    nz, nx, ny = material_id.shape
    slabs, tiles = lax.axis_size("gz"), lax.axis_size("xy")
    cells, tall, deep = nz * nx, nx * (nz + 2), nz + 2
    blocks = B_DEV * slabs * tiles
    field = cells * ny
    f32, bf16, i32 = jnp.float32, jnp.bfloat16, jnp.int32
    params = pltpu.CompilerParams(vmem_limit_bytes=24 * 1024 * 1024)
    raw = (material_eps, adjoint_e, adjoint_h, source_e, material_id, pml_level)
    raw = [pltpu.with_memory_space_constraint(a, pltpu.HBM) for a in raw]
    table = pltpu.SMEM(material_eps.shape, f32)
    z_msg, x_msg = shape_of(Z_SLOTS * nx, ny), shape_of(X_SLOTS * deep, ny)

    zb, za = pl.pallas_call(
        functools.partial(faces_kernel, nz, nx),
        out_shape=(z_msg, z_msg),
        in_specs=[HBM] * 6,
        out_specs=(VMEM,) * 2,
        scratch_shapes=[
            table,
            pltpu.VMEM((2, 3, 2, nx, ny), f32),
            pltpu.VMEM((2, 3, 2, nx, ny), f32),
            pltpu.VMEM((2, 3, 2, nx, ny), bf16),
            pltpu.VMEM((2, 2, nx, ny), i32),
            pltpu.VMEM((2, 2, nx, ny), i32),
            pltpu.SemaphoreType.DMA((11,)),
        ],
        compiler_params=params,
        cost_estimate=estimate(60 * field // 4, 4 * 4 * field),
        name="faces",
    )(*raw)

    zb = lax.ppermute(zb, "gz", swap_pairs(slabs, 1))
    za = lax.ppermute(za, "gz", swap_pairs(slabs, 0))

    work = pl.pallas_call(
        functools.partial(prepare_kernel, nz, nx),
        out_shape=shape_of(FIELDS * tall, ny),
        in_specs=[HBM] * 6,
        out_specs=VMEM,
        scratch_shapes=[
            table,
            pltpu.VMEM((nz, nx, ny), i32),
            pltpu.VMEM((nz, nx, ny), i32),
            pltpu.VMEM((3, nz, nx, ny), bf16),
            pltpu.VMEM((3, nz, nx, ny), f32),
            pltpu.VMEM((3, nz, nx, ny), f32),
            pltpu.SemaphoreType.DMA((6,)),
        ],
        compiler_params=params,
        cost_estimate=estimate(80 * field, 4 * 25 * field),
        name="prepare",
    )(*raw)

    zh, xb, xa = pl.pallas_call(
        functools.partial(columns_kernel, nz, nx),
        out_shape=(shape_of(20 * nx + 8, ny), x_msg, x_msg),
        in_specs=[VMEM] * 3,
        out_specs=(VMEM,) * 3,
        compiler_params=params,
        cost_estimate=estimate(4 * field, 4 * field),
        name="columns",
    )(zb, za, work)

    xb = lax.ppermute(xb, "xy", swap_pairs(tiles, 1))
    xa = lax.ppermute(xa, "xy", swap_pairs(tiles, 0))

    partial, edges = pl.pallas_call(
        functools.partial(interior_kernel, nz, nx, nz * slabs),
        out_shape=(shape_of(blocks, ny), shape_of(6 * deep, ny)),
        in_specs=[VMEM] * 4,
        out_specs=(VMEM,) * 2,
        scratch_shapes=[pltpu.VMEM((3 * tall, ny), f32)],
        compiler_params=params,
        cost_estimate=estimate(150 * field, 4 * 20 * field),
        name="interior",
    )(e_saved.reshape(-1, ny), work, zh, block_map)

    sums = pl.pallas_call(
        functools.partial(edge_kernel, nz, nx, nz * slabs),
        out_shape=shape_of(blocks, ny),
        in_specs=[VMEM] * 6,
        out_specs=VMEM,
        compiler_params=params,
        cost_estimate=estimate(4 * field, 4 * field),
        name="edges",
    )(work, partial, edges, block_map, xb, xa)

    gathered = lax.all_to_all(sums, ("gz", "xy"), 0, 0, tiled=True)

    field_e, field_h = pl.pallas_call(
        functools.partial(march_kernel, nz, nx),
        out_shape=(shape_of(3 * cells, ny), shape_of(3 * cells, ny)),
        in_specs=[VMEM] * 4,
        out_specs=(HBM, HBM),
        scratch_shapes=[
            pltpu.VMEM((10 * deep * 8, ny), f32),
            pltpu.VMEM((3 * cells, ny), f32),
            pltpu.VMEM((3 * cells, ny), f32),
            pltpu.SemaphoreType.DMA((6,)),
        ],
        compiler_params=params,
        cost_estimate=estimate(200 * field, 4 * 25 * field),
        name="march",
    )(work, zh, xb, xa)

    gathered = lax.all_to_all(sums, ("gz", "xy"), 0, 0, tiled=True)
    design_grad = jnp.sum(gathered.reshape(-1, B_DEV, ny), axis=(0, 2))
    return field_e.reshape(adjoint_e.shape), field_h.reshape(adjoint_h.shape), design_grad


def solution(mesh):
    placed = (
        P(None, "gz", "xy", None),
        P(None, "gz", "xy", None),
        P(None, "gz", "xy", None),
        P(None, None, "gz", "xy", None),
        P(),
        P("gz", "xy", None),
        P("gz", "xy", None),
        P("xy", None),
    )
    return jax.shard_map(
        on_device,
        mesh=mesh,
        in_specs=placed,
        out_specs=(P(None, "gz", "xy", None), P(None, "gz", "xy", None), P(("gz", "xy"))),
        check_vma=False,
    )
```

```python
import functools

import jax
import jax.numpy as jnp
from jax import lax
from jax.experimental import pallas as pl
from jax.experimental.pallas import tpu as pltpu
from jax.sharding import PartitionSpec as P

B_DEV = 2

DT_STEP = 0.5
SIGMA_UNIT = 0.15

V0, V1, V2, Q0, Q1, Q2, DR, H0, H1, H2, I0, I1, I2, DECAY, INV = range(15)
FIELDS = 15

Z_LOW = (H0, H1, H2, Q0, Q1, Q2, DR)
Z_HIGH = (V0, V1, V2, Q0, Q1, DR, H1, H2)
X_LOW = (H1, H2, Q0, Q1, Q2, DR)
X_HIGH = (V1, V2, Q1, Q2, DR)
EXTRA_Z = 7
EXTRA_X = 5
Z_SLOTS, X_SLOTS = 8, 6

VMEM = pl.BlockSpec(memory_space=pltpu.VMEM)
HBM = pl.BlockSpec(memory_space=pltpu.HBM)
ANY = pl.BlockSpec(memory_space=pl.ANY)


def shape_of(rows, ny):
    return jax.ShapeDtypeStruct((rows, ny), jnp.float32)


def is_odd(axis):
    return lax.rem(lax.axis_index(axis), 2) == 1


def either(odd, body, first, second):
    pl.when(jnp.logical_not(odd))(functools.partial(body, first, second))
    pl.when(odd)(functools.partial(body, second, first))


def masks(tall):
    row = lax.broadcasted_iota(jnp.int32, (tall, 128), 0)
    lane = lax.broadcasted_iota(jnp.int32, (tall, 128), 1)
    return row, lane == 0, lane == 127


def inverse_table(eps, nx):
    return [1.0 / jnp.full((nx, 128), eps[k], jnp.float32) for k in range(eps.shape[0])]


def cell_factors(kind, level, table):
    inv = table[0]
    for k in range(1, len(table)):
        inv = jnp.where(kind == k, table[k], inv)
    sigma = SIGMA_UNIT * level.astype(jnp.float32)
    recip = 1.0 / (1.0 + sigma)
    return (1.0 - sigma) * recip, DT_STEP * inv * recip, inv


def faces_kernel(nz, nx, eps_in, e_in, h_in, s_in, mat_in, pml_in, zb, za, eps, *rest):
    bufs, sems = rest[:-1], rest[-1]
    copies = [pltpu.make_async_copy(eps_in, eps, sems.at[0])]
    for k, ref in enumerate((e_in, h_in, s_in, mat_in, pml_in)):
        for side, start in enumerate((0, nz - 2)):
            part = pl.ds(start, 2)
            source = ref.at[:, part] if k < 3 else ref.at[part]
            copies.append(pltpu.make_async_copy(source, bufs[k].at[side], sems.at[len(copies)]))
    for copy in copies:
        copy.start()
    for copy in copies:
        copy.wait()
    e, h, s, mat, pml = bufs
    table = inverse_table(eps, nx)
    row, first, last = masks(nx)

    def next_y(f):
        return jnp.where(last, 0.0, pltpu.roll(f, 127, 1)) - f

    def next_x(f):
        return jnp.where(row == nx - 1, 0.0, pltpu.roll(f, nx - 1, 0)) - f

    def layer(side, z):
        decay, drive, _ = cell_factors(mat[side, z], pml[side, z], table)
        source = [s[side, c, z].astype(jnp.float32) for c in range(3)]
        incoming = [e[side, c, z] + source[c] for c in range(3)]
        v = [drive * f for f in incoming]
        q = [decay * f + g for f, g in zip(incoming, source)]
        return v, q, drive, [h[side, c, z] for c in range(3)]

    v, q, drive, mag = layer(1, 1)
    w, _, _, deep = layer(1, 0)
    deep_x = deep[0] + (next_y(w[2]) - (v[1] - w[1]))
    deep_y = deep[1] + ((v[0] - w[0]) - next_x(w[2]))
    low = [
        mag[0] + (next_y(v[2]) + v[1]),
        mag[1] - (v[0] + next_x(v[2])),
        mag[2] + (next_x(v[1]) - next_y(v[0])),
        q[0] - DT_STEP * deep_y,
        q[1] + DT_STEP * deep_x,
        q[2],
        drive,
        jnp.where(row == 0, v[1][:1], jnp.where(row == 1, v[2][:1], w[2][:1])),
    ]
    v, q, drive, mag = layer(0, 0)
    w, _, _, _ = layer(0, 1)
    edge_x = mag[0] + (next_y(v[2]) - (w[1] - v[1]))
    edge_y = mag[1] + (w[0] - v[0])
    high = [v[0], v[1], v[2], q[0], q[1] - DT_STEP * edge_x, drive, edge_y, mag[2]]

    def put(top, bottom):
        for slot in range(Z_SLOTS):
            top[pl.ds(slot * nx, nx), :] = low[slot]
            bottom[pl.ds(slot * nx, nx), :] = high[slot]

    either(is_odd("gz"), put, za, zb)


def prepare_kernel(nz, nx, eps_in, e_in, h_in, s_in, mat_in, pml_in, work, eps, *rest):
    bufs, sems = rest[:-1], rest[-1]
    copies = [
        pltpu.make_async_copy(source, target, sems.at[k])
        for k, (source, target) in enumerate(
            zip((eps_in, mat_in, pml_in, s_in, e_in, h_in), (eps,) + bufs)
        )
    ]
    for copy in copies:
        copy.start()
    mat, pml, s, e, h = bufs
    for copy in copies[:5]:
        copy.wait()
    table = inverse_table(eps, nx)
    tall = nx * (nz + 2)
    for z in range(nz):
        decay, drive, inv = cell_factors(mat[z], pml[z], table)

        def keep(field, value):
            work[pl.ds(field * tall + (z + 1) * nx, nx), :] = value

        keep(DR, drive)
        keep(DECAY, decay)
        keep(INV, inv)
        for c in range(3):
            source = s[c, z].astype(jnp.float32)
            incoming = e[c, z] + source
            keep(V0 + c, drive * incoming)
            keep(Q0 + c, decay * incoming + source)
            keep(I0 + c, incoming)
    copies[5].wait()
    for c in range(3):
        for z in range(nz):
            work[pl.ds((H0 + c) * tall + (z + 1) * nx, nx), :] = h[c, z]


def columns_kernel(nz, nx, zb, za, work, zh, xb, xa):
    tall = nx * (nz + 2)
    deep = nz + 2
    zero = jnp.zeros((nx, 128), jnp.float32)

    def take(low, high):
        for field in range(V0, H2 + 1):
            for k, (slots, ref) in enumerate(((Z_LOW, low), (Z_HIGH, high))):
                at = pl.ds((2 * field + k) * nx, nx)
                if field in slots:
                    zh[at, :] = ref[pl.ds(slots.index(field) * nx, nx), :]
                else:
                    zh[at, :] = zero

    odd_z = is_odd("gz")
    either(odd_z, take, zb, za)
    index = jnp.where(odd_z, 0, 1)
    row, first, last = masks(deep)

    def extra(k):
        at = pl.ds(EXTRA_Z * nx + k, 1)
        return jnp.where(jnp.broadcast_to(index, (1, 128)) == 0, za[at, :], zb[at, :])

    for k in range(2):
        zh[pl.ds(20 * nx + k, 1), :] = extra(k)

    def next_y(f):
        return jnp.where(last, 0.0, pltpu.roll(f, 127, 1)) - f

    def prev_y(f):
        return f - jnp.where(first, 0.0, pltpu.roll(f, 1, 1))

    def next_z(f):
        return jnp.where(row == deep - 1, 0.0, pltpu.roll(f, deep - 1, 0) - f)

    def prev_z(f):
        return f - jnp.where(row == 0, 0.0, pltpu.roll(f, 1, 0))

    def column(field, x):
        own = work[pl.ds(field * tall + x, deep, stride=nx), :]
        below, above = (zh[pl.ds((2 * field + k) * nx + x, 1), :] for k in range(2))
        return jnp.where(row == 0, below, jnp.where(row == deep - 1, above, own))

    bottom_edge = jnp.logical_and(row == 0, jnp.broadcast_to(lax.axis_index("gz"), row.shape) == 0)

    x = nx - 1
    v = [column(V0 + c, x) for c in range(3)]
    w = [column(V0 + c, x - 1) for c in range(3)]
    mag_x = column(H0, x) + (next_y(v[2]) - next_z(v[1]))
    mag_x = jnp.where(bottom_edge, 0.0, mag_x)
    deep_y = column(H1, x - 1) + (next_z(w[0]) - (v[2] - w[2]))
    deep_z = column(H2, x - 1) + ((v[1] - w[1]) - next_y(w[0]))
    low = [
        column(H1, x) + (next_z(v[0]) + v[2]),
        column(H2, x) - (v[1] + next_y(v[0])),
        column(Q0, x),
        column(Q1, x) - DT_STEP * (prev_z(mag_x) + deep_z),
        column(Q2, x) + DT_STEP * (deep_y + prev_y(mag_x)),
        column(DR, x),
    ]

    v = [column(V0 + c, 0) for c in range(3)]
    w = [column(V0 + c, 1) for c in range(3)]
    mag_x = column(H0, 0) + (next_y(v[2]) - next_z(v[1]))
    mag_x = jnp.where(bottom_edge, 0.0, mag_x)
    mag_y = column(H1, 0) + (next_z(v[0]) - (w[2] - v[2]))
    mag_z = column(H2, 0) + ((w[1] - v[1]) - next_y(v[0]))
    high = [
        jnp.where(row == 0, extra(0), v[1]),
        jnp.where(row == 0, extra(1), v[2]),
        column(Q1, 0) - DT_STEP * (prev_z(mag_x) - mag_z),
        column(Q2, 0) - DT_STEP * (mag_y - prev_y(mag_x)),
        column(DR, 0),
        jnp.broadcast_to(extra(2), (deep, 128)),
    ]

    def put(top, bottom):
        for slot in range(X_SLOTS):
            top[pl.ds(slot * deep, deep), :] = low[slot]
            bottom[pl.ds(slot * deep, deep), :] = high[slot]

    either(is_odd("xy"), put, xa, xb)


def spread(fours, groups, blocks, shape):
    owner = lax.broadcasted_iota(jnp.int32, shape, 0)
    out = jnp.zeros(shape, jnp.float32)
    for four, group in zip(fours, groups):
        out = out + jnp.where(blocks[pl.ds(4 * group, 1), :] == owner, four, 0.0)
    return out


def interior_kernel(nz, nx, layers, saved, work, zh, blocks, partial, edges, weight):
    cells, tall = nz * nx, nx * (nz + 2)
    row, first, last = masks(nx)
    above_edge = jnp.broadcast_to(lax.axis_index("gz"), row.shape) > 0

    def load(field, z):
        if 0 <= z < nz:
            return work[pl.ds(field * tall + (z + 1) * nx, nx), :]
        return zh[pl.ds((2 * field + (z > 0)) * nx, nx), :]

    def next_y(f):
        return jnp.where(last, 0.0, pltpu.roll(f, 127, 1)) - f

    def prev_y(f):
        return f - jnp.where(first, 0.0, pltpu.roll(f, 1, 1))

    def next_x(f):
        return jnp.where(row == nx - 1, 0.0, pltpu.roll(f, nx - 1, 0)) - f

    def prev_x(f):
        return f - jnp.where(row == 0, 0.0, pltpu.roll(f, 1, 0))

    total = jnp.zeros((nx, 128), jnp.float32)
    here = [load(V0 + c, -1) for c in range(3)]
    below = None
    for z in range(-1, nz):
        above = [load(V0 + c, z + 1) for c in range(3)]
        mag = [
            load(H0, z) + (next_y(here[2]) - (above[1] - here[1])),
            load(H1, z) + ((above[0] - here[0]) - next_x(here[2])),
        ]
        if z < 0:
            mag = [jnp.where(above_edge, f, 0.0) for f in mag]
        else:
            mag.append(load(H2, z) + (next_x(here[1]) - next_y(here[0])))
            curl = [
                prev_y(mag[2]) - (mag[1] - below[1]),
                (mag[0] - below[0]) - prev_x(mag[2]),
                prev_x(mag[1]) - prev_y(mag[0]),
            ]
            decay, inv = load(DECAY, z), load(INV, z)
            cell = jnp.zeros((nx, 128), jnp.float32)
            for c in range(3):
                times = [
                    saved[pl.ds((3 * t + c) * cells + z * nx, nx), :].astype(jnp.float32)
                    for t in range(3)
                ]
                factor = times[1] - decay * times[0]
                weight[pl.ds(c * tall + (z + 1) * nx, nx), :] = factor * inv
                cell = cell + load(I0 + c, z) * (times[2] - decay * times[1])
                cell = cell + (load(Q0 + c, z) - DT_STEP * curl[c]) * factor
            total = total + cell * inv
        here, below = above, mag
    total = total * (-1.0 / layers)
    fours = [
        jnp.sum(total[4 * k : 4 * k + 4], axis=0, keepdims=True) for k in range(nx // 4)
    ]
    partial[...] = spread(fours, range(nx // 4), blocks, partial.shape)
    for side, x in enumerate((0, nx - 1)):
        for c in range(3):
            part = weight[pl.ds(c * tall + nx + x, nz, stride=nx), :]
            edges[pl.ds((3 * side + c) * (nz + 2) + 1, nz), :] = part


def march(nz, nx, work, zh, xb, xa, e_out, h_out, xh, out_e, out_h, sems):
    cells, tall, deep = nz * nx, nx * (nz + 2), nz + 2
    index_z, index_x = lax.axis_index("gz"), lax.axis_index("xy")
    odd_x = is_odd("xy")
    xh[...] = jnp.zeros_like(xh)

    def take(low, high):
        for slots, ref, place in ((X_LOW, low, 7), (X_HIGH, high, 0)):
            for slot, field in enumerate(slots):
                at = pl.ds(field * deep * 8 + place, deep, stride=8)
                xh[at, :] = ref[pl.ds(slot * deep, deep), :]

    either(odd_x, take, xb, xa)
    at = pl.ds(EXTRA_X * deep, 1)
    beyond = jnp.where(jnp.broadcast_to(odd_x, (1, 128)), xb[at, :], xa[at, :])

    rows = nx + 8
    row, first, last = masks(rows)
    inside_x = jnp.logical_or(
        row < nx, jnp.logical_and(row == rows - 1, jnp.broadcast_to(index_x, row.shape) > 0)
    )
    inside_z = jnp.logical_and(inside_x, jnp.broadcast_to(index_z, row.shape) > 0)

    def load(field, z):
        if 0 <= z < nz:
            own = work[pl.ds(field * tall + (z + 1) * nx, nx), :]
        else:
            own = zh[pl.ds((2 * field + (z > 0)) * nx, nx), :]
        side = xh[pl.ds((field * deep + z + 1) * 8, 8), :]
        return jnp.concatenate([own, side], axis=0)

    def next_y(f):
        return jnp.where(last, 0.0, pltpu.roll(f, 127, 1)) - f

    def prev_y(f):
        return f - jnp.where(first, 0.0, pltpu.roll(f, 1, 1))

    def next_x(f):
        return pltpu.roll(f, rows - 1, 0) - f

    def prev_x(f):
        return f - pltpu.roll(f, 1, 0)

    def magnetic(z, old, here, above):
        keep = inside_z if z < 0 else inside_x
        out = [
            old[0] + (next_y(here[2]) - (above[1] - here[1])),
            old[1] + ((above[0] - here[0]) - next_x(here[2])),
            old[2] + (next_x(here[1]) - next_y(here[0])),
        ]
        return [jnp.where(keep, f, 0.0) for f in out]

    def curl_p(here, below):
        return [
            prev_y(here[2]) - (here[1] - below[1]),
            (here[0] - below[0]) - prev_x(here[2]),
            prev_x(here[1]) - prev_y(here[0]),
        ]

    def flush(z):
        for c in range(3):
            at = pl.ds(c * cells + z * nx, nx * 2)
            for k, (source, target) in enumerate(((out_e, e_out), (out_h, h_out))):
                sem = sems.at[k * 3 + c]
                pltpu.make_async_copy(source.at[at, :], target.at[at, :], sem).start()

    zeros = jnp.zeros((rows, 128), jnp.float32)
    v_here = [load(V0 + c, -1) for c in range(3)]
    mag_below = [zeros] * 3
    mag_mid = mag2_below = inc_below = drv_below = None
    for z in range(-1, nz + 1):
        v_above = [load(V0 + c, z + 1) for c in range(3)] if z < nz else v_here
        old = [load(H0 + c, z) for c in range(3)]
        if z < 0:
            side_y, side_z = (zh[pl.ds(20 * nx + k, 1), :] for k in range(2))
            old[1] = old[1] - jnp.where(row == rows - 1, side_z, 0.0)
            old[2] = old[2] + jnp.where(row == rows - 1, side_y, 0.0)
        mag = magnetic(z, old, v_here, v_above)
        if z == nz:
            mag[0] = zeros
        v_here = v_above
        curl = curl_p(mag, mag_below)
        inc = [load(Q0 + c, z) - DT_STEP * curl[c] for c in range(3)]
        if z < 0:
            inc[0] = inc[0] + jnp.where(row == nx - 1, DT_STEP * beyond, 0.0)
        drive = load(DR, z)
        drv = [drive * f for f in inc]
        if z >= 0:
            low = z - 1
            mag2 = magnetic(low, mag_mid, drv_below, drv)
            if low >= 0:
                decay = work[pl.ds(DECAY * tall + (low + 1) * nx, nx), :]
                curl = curl_p(mag2, mag2_below)
                for c in range(3):
                    at = pl.ds(c * cells + low * nx, nx)
                    out_h[at, :] = mag2[c][:nx]
                    out_e[at, :] = decay * inc_below[c][:nx] - DT_STEP * curl[c][:nx]
                if low % 2 == 1:
                    flush(low - 1)
            mag2_below = mag2
        inc_below, drv_below = inc, drv
        mag_mid, mag_below = mag, mag

    for c in range(3):
        at = pl.ds(c * cells, cells)
        for k, (source, target) in enumerate(((out_e, e_out), (out_h, h_out))):
            pltpu.make_async_copy(source.at[at, :], target.at[at, :], sems.at[k * 3 + c]).wait()


def edge_kernel(
    nz, nx, layers, work, zh, partial, edges, blocks, xb, xa, sums, e_out, h_out, *scratch
):
    tall, deep = nx * (nz + 2), nz + 2
    row, first, last = masks(deep)
    odd_x = jnp.broadcast_to(is_odd("xy"), row.shape)
    own = jnp.logical_and(row > 0, row < deep - 1)
    low_side = jnp.logical_and(own, jnp.broadcast_to(lax.axis_index("xy"), row.shape) > 0)

    def slot(slots, field):
        at = pl.ds(slots.index(field) * deep, deep)
        return jnp.where(odd_x, xa[at, :], xb[at, :]), jnp.where(odd_x, xb[at, :], xa[at, :])

    def prev_y(f):
        return f - jnp.where(first, 0.0, pltpu.roll(f, 1, 1))

    def factor(side, c):
        return edges[pl.ds((3 * side + c) * deep, deep), :]

    mag_y = slot(X_LOW, H1)[0] - work[pl.ds(V2 * tall, deep, stride=nx), :]
    mag_z = slot(X_LOW, H2)[0] + work[pl.ds(V1 * tall, deep, stride=nx), :]
    near = DT_STEP * (mag_y * factor(0, 2) - mag_z * factor(0, 1))
    v_y, v_z = slot(X_HIGH, V1)[1], slot(X_HIGH, V2)[1]
    far = DT_STEP * (
        v_y * factor(1, 1)
        + v_z * factor(1, 2)
        - (prev_y(v_y) + (v_z - pltpu.roll(v_z, 1, 0))) * factor(1, 0)
    )
    near = jnp.sum(jnp.where(low_side, near, 0.0), axis=0, keepdims=True)
    far = jnp.sum(jnp.where(own, far, 0.0), axis=0, keepdims=True)

    ends = (near * (-1.0 / layers), far * (-1.0 / layers))
    sums[...] = partial[...] + spread(ends, (0, nx // 4 - 1), blocks, sums.shape)

    @pl.when(waits_long())
    def _():
        march(nz, nx, work, zh, xb, xa, e_out, h_out, *scratch)


def late_kernel(nz, nx, work, zh, xb, xa, gathered, e_in, h_in, e_out, h_out, *scratch):
    @pl.when(jnp.logical_not(waits_long()))
    def _():
        march(nz, nx, work, zh, xb, xa, e_out, h_out, *scratch)


def waits_long():
    return lax.axis_index("xy") * 8 < lax.axis_size("xy")


def swap_pairs(count, offset):
    pairs = []
    for low in range(offset, count - 1, 2):
        pairs += [(low, low + 1), (low + 1, low)]
    return pairs


def estimate(flops, moved):
    return pl.CostEstimate(flops=flops, bytes_accessed=moved, transcendentals=0)


def on_device(
    adjoint_e, adjoint_h, source_e, e_saved, material_eps, material_id, pml_level, block_map
):
    nz, nx, ny = material_id.shape
    slabs, tiles = lax.axis_size("gz"), lax.axis_size("xy")
    cells, tall, deep = nz * nx, nx * (nz + 2), nz + 2
    blocks = B_DEV * slabs * tiles
    field = cells * ny
    f32, bf16, i32 = jnp.float32, jnp.bfloat16, jnp.int32
    params = pltpu.CompilerParams(vmem_limit_bytes=24 * 1024 * 1024)
    raw = (material_eps, adjoint_e, adjoint_h, source_e, material_id, pml_level)
    raw = [pltpu.with_memory_space_constraint(a, pltpu.HBM) for a in raw]
    table = pltpu.SMEM(material_eps.shape, f32)
    z_msg, x_msg = shape_of(Z_SLOTS * nx, ny), shape_of(X_SLOTS * deep, ny)

    zb, za = pl.pallas_call(
        functools.partial(faces_kernel, nz, nx),
        out_shape=(z_msg, z_msg),
        in_specs=[HBM] * 6,
        out_specs=(VMEM,) * 2,
        scratch_shapes=[
            table,
            pltpu.VMEM((2, 3, 2, nx, ny), f32),
            pltpu.VMEM((2, 3, 2, nx, ny), f32),
            pltpu.VMEM((2, 3, 2, nx, ny), bf16),
            pltpu.VMEM((2, 2, nx, ny), i32),
            pltpu.VMEM((2, 2, nx, ny), i32),
            pltpu.SemaphoreType.DMA((11,)),
        ],
        compiler_params=params,
        cost_estimate=estimate(60 * field // 4, 4 * 4 * field),
        name="faces",
    )(*raw)

    zb = lax.ppermute(zb, "gz", swap_pairs(slabs, 1))
    za = lax.ppermute(za, "gz", swap_pairs(slabs, 0))

    work = pl.pallas_call(
        functools.partial(prepare_kernel, nz, nx),
        out_shape=shape_of(FIELDS * tall, ny),
        in_specs=[HBM] * 6,
        out_specs=VMEM,
        scratch_shapes=[
            table,
            pltpu.VMEM((nz, nx, ny), i32),
            pltpu.VMEM((nz, nx, ny), i32),
            pltpu.VMEM((3, nz, nx, ny), bf16),
            pltpu.VMEM((3, nz, nx, ny), f32),
            pltpu.VMEM((3, nz, nx, ny), f32),
            pltpu.SemaphoreType.DMA((6,)),
        ],
        compiler_params=params,
        cost_estimate=estimate(80 * field, 4 * 25 * field),
        name="prepare",
    )(*raw)

    zh, xb, xa = pl.pallas_call(
        functools.partial(columns_kernel, nz, nx),
        out_shape=(shape_of(20 * nx + 8, ny), x_msg, x_msg),
        in_specs=[VMEM] * 3,
        out_specs=(VMEM,) * 3,
        compiler_params=params,
        cost_estimate=estimate(4 * field, 4 * field),
        name="columns",
    )(zb, za, work)

    xb = lax.ppermute(xb, "xy", swap_pairs(tiles, 1))
    xa = lax.ppermute(xa, "xy", swap_pairs(tiles, 0))

    partial, edges = pl.pallas_call(
        functools.partial(interior_kernel, nz, nx, nz * slabs),
        out_shape=(shape_of(blocks, ny), shape_of(6 * deep, ny)),
        in_specs=[VMEM] * 4,
        out_specs=(VMEM,) * 2,
        scratch_shapes=[pltpu.VMEM((3 * tall, ny), f32)],
        compiler_params=params,
        cost_estimate=estimate(150 * field, 4 * 20 * field),
        name="interior",
    )(e_saved.reshape(-1, ny), work, zh, block_map)

    fields = (shape_of(3 * cells, ny), shape_of(3 * cells, ny))
    scratch = [
        pltpu.VMEM((10 * deep * 8, ny), f32),
        pltpu.VMEM((3 * cells, ny), f32),
        pltpu.VMEM((3 * cells, ny), f32),
        pltpu.SemaphoreType.DMA((6,)),
    ]
    sums, field_e, field_h = pl.pallas_call(
        functools.partial(edge_kernel, nz, nx, nz * slabs),
        out_shape=(shape_of(blocks, ny),) + fields,
        in_specs=[VMEM] * 7,
        out_specs=(VMEM, HBM, HBM),
        scratch_shapes=scratch,
        compiler_params=params,
        cost_estimate=estimate(4 * field, 4 * field),
        name="edges",
    )(work, zh, partial, edges, block_map, xb, xa)

    gathered = lax.all_to_all(sums, ("gz", "xy"), 0, 0, tiled=True)

    field_e, field_h = pl.pallas_call(
        functools.partial(late_kernel, nz, nx),
        out_shape=fields,
        in_specs=[VMEM] * 4 + [ANY, HBM, HBM],
        out_specs=(HBM, HBM),
        input_output_aliases={5: 0, 6: 1},
        scratch_shapes=scratch,
        compiler_params=params,
        cost_estimate=estimate(200 * field, 4 * 25 * field),
        name="fields",
    )(work, zh, xb, xa, gathered, field_e, field_h)

    design_grad = jnp.sum(gathered.reshape(-1, B_DEV, ny), axis=(0, 2))
    return field_e.reshape(adjoint_e.shape), field_h.reshape(adjoint_h.shape), design_grad


def solution(mesh):
    placed = (
        P(None, "gz", "xy", None),
        P(None, "gz", "xy", None),
        P(None, "gz", "xy", None),
        P(None, None, "gz", "xy", None),
        P(),
        P("gz", "xy", None),
        P("gz", "xy", None),
        P("xy", None),
    )
    return jax.shard_map(
        on_device,
        mesh=mesh,
        in_specs=placed,
        out_specs=(P(None, "gz", "xy", None), P(None, "gz", "xy", None), P(("gz", "xy"))),
        check_vma=False,
    )
```
